32 devices in a mesh: sect: 2 (over core), exp: 8 (over z, x), tp: 2 (over y).
Axes of the slice: x: 2, y: 2, z: 4, core: 2. Of those that a mesh axis runs over, the one named last changes fastest.
Arguments:
- tokens: bfloat16 [256, 6144], P(('sect', 'exp', 'tp')), may hold values from -6 to 6
- router_logits: float32 [256, 2], P(('sect', 'exp', 'tp')), may hold values from -6 to 6
- expert_ids: int32 [256, 2], P(('sect', 'exp', 'tp')), may hold values from 0 to 3, all different within a row; in each aligned block of 8 rows (0 to 7, 8 to 15, ...) at most 8 rows name the same one
- w_gate: bfloat16 [16, 6144, 2048], P(('sect', 'exp'), None, 'tp'), may hold values from -0.078125 to 0.078125
- w_up: bfloat16 [16, 6144, 2048], P(('sect', 'exp'), None, 'tp'), may hold values from -0.078125 to 0.078125
- w_down: bfloat16 [16, 2048, 6144], P(('sect', 'exp'), 'tp'), may hold values from -0.0625 to 0.0625
Outputs:
- mixture: bfloat16 [256, 6144], P(('sect', 'exp', 'tp'))
The draws below stay inside these ranges and needn't reach their ends.
Inputs may be any that keep to these rules, and one draw needn't show every extreme that they name: `expert_ids`: each token names two different experts. Among the 8 tokens of one device no expert is named more than 8 times, and in every draw some expert is named exactly 8 times by the tokens of some device.
All inputs are finite; a program needn't handle non-finite values.
Results may differ from the reference program's by a relative error of at most 0.0049.
Values may be sent and summed in bfloat16 or wider, within the bound.
No kernel may reach another device: no remote copies, remote signals or barrier semaphores. Data moves between devices by JAX's collectives and lax.ppermute only.
A program may use at most 128 MiB of HBM per device.

```python
import math
import jax
import jax.numpy as jnp
import numpy as np
from jax import lax

D = 6144
FF = 8192
TOK_DEV = 8
EXPERTS = 4
FFP = 2048
CAP = 8
TOKENS = 256
DEVICES = 32


def block_scale(key, extent, pieces, smallest, largest):
    level = 1.0
    for axis_at, parts in pieces:
        heights = jax.random.uniform(jax.random.fold_in(jax.random.fold_in(key, 6), axis_at), (parts,), jnp.float32, smallest / len(pieces), largest / len(pieces))
        level = level * jnp.repeat(jnp.exp(heights), extent[axis_at] // parts).reshape((-1,) + (1,) * (len(extent) - 1 - axis_at))
    return level


def deal_out(stream_key, own, number, rows, count, top, most, skew):
    ranking = jax.random.permutation(stream_key, count)
    crowded, usual = load_shares(count, rows * top, most, skew, True), load_shares(count, rows * top, most, skew, False)
    places = jnp.arange(count)

    def named(tallies, turn):
        used = int((tallies > 0).sum())
        fixed = max(1, used // 4)
        shifted = fixed + (places - fixed + turn * (used - fixed)) % max(1, count - fixed)
        return jnp.zeros((count,), jnp.int32).at[ranking[jnp.where(places < fixed, places, shifted)]].set(jnp.asarray(tallies, jnp.int32))

    tallies = jnp.where(number % 4 == 0, named(crowded, number // 4), named(usual, number - number // 4 - 1))
    mixed = jax.random.permutation(jax.random.fold_in(own, 3), count)
    source_of, taker = mixed[0:count // 2 * 2:2], mixed[1:count // 2 * 2:2]
    slack = jnp.minimum(tallies[source_of] - 1, most - tallies[taker]) // 2
    slack = jnp.where((source_of == ranking[0]) | (taker == ranking[0]) | (tallies[taker] == 0), 0, jnp.maximum(slack, 0))
    shifted = jax.random.randint(jax.random.fold_in(own, 4), (count // 2,), 0, 1 << 20) % (slack + 1)
    tallies = tallies.at[source_of].add(-shifted).at[taker].add(shifted)
    items = jnp.searchsorted(jnp.cumsum(tallies), jnp.arange(rows * top), side="right").astype(jnp.int32)
    grid = items.reshape(top, rows).T
    grid = grid[jax.random.permutation(jax.random.fold_in(own, 1), rows)]
    turn = jax.random.randint(jax.random.fold_in(own, 2), (rows, 1), 0, top)
    return jnp.take_along_axis(grid, (jnp.arange(top)[None, :] + turn) % top, axis=1)


def load_shares(amount, total, bound, skew, full):
    portions = [(1 << 20) // math.isqrt(grade ** skew) + 1 for grade in range(1, amount + 1)]
    largest = bound if full else min(bound, max(-(-total // amount), total * portions[0] // sum(portions)))
    least = 1 if total - largest >= amount - 1 else 0
    holding, spare = [largest] + [least] * (amount - 1), total - largest - least * (amount - 1)
    while spare > 0:
        candidates = [i for i in range(1, amount) if holding[i] < largest] or [i for i in range(1, amount) if holding[i] < bound]
        mass, remaining = sum([portions[i] for i in candidates]), spare
        for i in candidates:
            extra = min(bound - holding[i], max(1, remaining * portions[i] // mass), spare)
            holding[i] = holding[i] + extra
            spare = spare - extra
    return np.array(holding)


def gaussian(stream_key, dims, width, most, split=(), held_as=jnp.bfloat16):
    gain = block_scale(stream_key, dims, split, -0.22, 0.18) if split else 1.0
    values = jax.random.normal(stream_key, dims, jnp.float32) * width * gain
    return jnp.minimum(jnp.maximum(values, -most), most).astype(held_as)


def setup_inputs(seed: int = 0) -> dict:
    key_list = jax.random.split(jax.random.key(seed), 7)
    tokens = gaussian(key_list[0], (TOKENS, D), 1.0, 6.0, ((0, 32),))
    router_logits = gaussian(key_list[1], (TOKENS, 2), 1.5, 6.0, ((0, 32),), jnp.float32)
    expert_ids_keys = jax.random.split(jax.random.fold_in(key_list[2], 1), TOKENS // TOK_DEV)
    expert_ids_turns = jax.random.permutation(jax.random.fold_in(key_list[2], 3), TOKENS // TOK_DEV)
    expert_ids = jax.vmap(lambda own, number: deal_out(jax.random.fold_in(key_list[2], 2), own, number, TOK_DEV, EXPERTS, 2, CAP, 2))(expert_ids_keys, expert_ids_turns).reshape((TOKENS, 2))
    w_gate = gaussian(key_list[3], (EXPERTS * 4, D, FFP), D ** -0.5, 0.078125, ((0, 16), (2, 2)))
    w_up = gaussian(key_list[4], (EXPERTS * 4, D, FFP), D ** -0.5, 0.078125, ((0, 16), (2, 2)))
    w_down = gaussian(key_list[5], (EXPERTS * 4, FFP, D), FF ** -0.5, 0.0625, ((0, 16), (1, 2)))
    return dict(tokens=tokens, router_logits=router_logits, expert_ids=expert_ids, w_gate=w_gate, w_up=w_up, w_down=w_down)


def place_slots(ids_block, experts):
    flat_ids = ids_block.reshape(-1)
    hits_mask = (flat_ids[:, None] == jnp.arange(experts, dtype=jnp.int32)[None, :]).astype(jnp.int32)
    earlier = jnp.cumsum(hits_mask, axis=0) - hits_mask
    slot_rank = jnp.sum(earlier * hits_mask, axis=1).astype(jnp.int32)
    return flat_ids.astype(jnp.int32), slot_rank


def expert_ffn(row_block, gate_part, up_part, down_part):
    summed = jnp.zeros((row_block.shape[0], down_part.shape[2]), jnp.float32)
    for quarter in range(4):
        gate_proj = jnp.dot(row_block, gate_part[quarter], preferred_element_type=jnp.float32)
        up_proj = jnp.dot(row_block, up_part[quarter], preferred_element_type=jnp.float32)
        hidden = (jax.nn.silu(gate_proj) * up_proj).astype(jnp.bfloat16)
        summed = summed + jnp.dot(hidden, down_part[quarter], preferred_element_type=jnp.float32)
    return summed


def reference(tokens, router_logits, expert_ids, w_gate, w_up, w_down):
    blocks = expert_ids.reshape(DEVICES, TOK_DEV * 2)
    flat_ids, slot_rank = jax.vmap(lambda b: place_slots(b, EXPERTS))(blocks)
    device_pos = jnp.arange(DEVICES, dtype=jnp.int32)[:, None]
    target = (flat_ids * (DEVICES * CAP) + device_pos * CAP + slot_rank).reshape(-1).astype(jnp.int32)
    repeated = jnp.repeat(tokens, 2, axis=0)
    slab_rows = jnp.zeros((EXPERTS * DEVICES * CAP, D), jnp.bfloat16).at[target].set(repeated)
    slab_rows = slab_rows.reshape(EXPERTS, DEVICES * CAP, D)

    def one_expert(expert):
        gate_part = lax.dynamic_slice_in_dim(w_gate, expert * 4, 4, 0)
        up_part = lax.dynamic_slice_in_dim(w_up, expert * 4, 4, 0)
        down_part = lax.dynamic_slice_in_dim(w_down, expert * 4, 4, 0)
        row_block = lax.dynamic_index_in_dim(slab_rows, expert, 0, keepdims=False)
        return expert_ffn(row_block, gate_part, up_part, down_part)

    outputs = lax.map(one_expert, jnp.arange(EXPERTS, dtype=jnp.int32)).reshape(EXPERTS * DEVICES * CAP, D)
    weights = jax.nn.sigmoid(router_logits - router_logits[:, ::-1]).reshape(-1)
    picked = outputs[target] * weights[:, None]
    mixture = jnp.sum(picked.reshape(TOKENS, 2, D), axis=1)
    return mixture.astype(jnp.bfloat16)
```

```python
import jax
import jax.numpy as jnp
from jax import lax
from jax.experimental import pallas as pl
from jax.experimental.pallas import tpu as pltpu
from jax.sharding import PartitionSpec as P

AXES = ("sect", "exp", "tp")
CHUNKS = 2
LANES = 128
VMEM = pl.BlockSpec(memory_space=pltpu.VMEM)


def gate_up_kernel(depth, part_count, has_prev, *refs):
    parts = refs[:part_count]
    wg_ref, wu_ref = refs[part_count : part_count + 2]
    rest = refs[part_count + 2 :]
    rows = jnp.concatenate([p[:, :depth] for p in parts], axis=0)
    gate = jnp.dot(rows, wg_ref[0], preferred_element_type=jnp.float32)
    up = jnp.dot(rows, wu_ref[0], preferred_element_type=jnp.float32)
    if has_prev:
        gate = gate + rest[0][...]
        up = up + rest[1][...]
        rest = rest[2:]
    if len(rest) == 1:
        rest[0][...] = (gate / (1.0 + jnp.exp(-gate)) * up).astype(jnp.bfloat16)
    else:
        rest[0][...] = gate
        rest[1][...] = up


def gate_up(parts, w_gate, w_up, chunk, depth, prev, last):
    row_count = sum(p.shape[0] for p in parts)
    width = w_gate.shape[2]
    tile = 256
    weight_spec = pl.BlockSpec((1, depth, tile), lambda i: (0, chunk, i))
    tile_spec = pl.BlockSpec((row_count, tile), lambda i: (0, i))
    out_types = [jnp.bfloat16] if last else [jnp.float32, jnp.float32]
    return pl.pallas_call(
        lambda *refs: gate_up_kernel(depth, len(parts), bool(prev), *refs),
        grid=(width // tile,),
        in_specs=[VMEM] * len(parts) + [weight_spec] * 2 + [tile_spec] * len(prev),
        out_specs=[tile_spec] * len(out_types),
        out_shape=[jax.ShapeDtypeStruct((row_count, width), t) for t in out_types],
        cost_estimate=pl.CostEstimate(
            flops=4 * row_count * depth * width,
            bytes_accessed=4 * depth * width,
            transcendentals=row_count * width if last else 0,
        ),
        compiler_params=pltpu.CompilerParams(vmem_limit_bytes=40 << 20),
        name="gate_up",
    )(*parts, w_gate, w_up, *prev)


def down_kernel(pick_ref, hidden_ref, wd_ref, mine_ref, other_ref, keep_ref, send_ref):
    out = jnp.dot(hidden_ref[...], wd_ref[0], preferred_element_type=jnp.float32)
    half = keep_ref.shape[0]
    columns = mine_ref.shape[1] - LANES

    def share(ref):
        shares = ref[:, columns:].astype(jnp.float32)
        return jnp.sum(shares * pick_ref[...], axis=1, keepdims=True)

    keep_ref[...] = out[:half] * share(mine_ref)
    send_ref[...] = (out[half:] * share(other_ref)).astype(jnp.bfloat16)


def down(pick, hidden, w_down, mine, other, chunk, chunk_width):
    row_count, depth = hidden.shape
    half = row_count // 2
    tile = 512
    first = chunk * (chunk_width // tile)
    return pl.pallas_call(
        down_kernel,
        grid=(chunk_width // tile,),
        in_specs=[
            VMEM,
            VMEM,
            pl.BlockSpec((1, depth, tile), lambda i: (0, 0, first + i)),
            VMEM,
            VMEM,
        ],
        out_specs=[pl.BlockSpec((half, tile), lambda i: (0, i))] * 2,
        out_shape=[
            jax.ShapeDtypeStruct((half, chunk_width), jnp.float32),
            jax.ShapeDtypeStruct((half, chunk_width), jnp.bfloat16),
        ],
        cost_estimate=pl.CostEstimate(
            flops=2 * row_count * depth * chunk_width,
            bytes_accessed=2 * depth * chunk_width,
            transcendentals=0,
        ),
        compiler_params=pltpu.CompilerParams(vmem_limit_bytes=40 << 20),
        name="down",
    )(pick, hidden, w_down, mine, other)


def share_columns(router_logits, expert_ids, experts):
    weights = jax.nn.sigmoid(router_logits - router_logits[:, ::-1])
    named = expert_ids[:, :, None] == jnp.arange(experts, dtype=jnp.int32)[None, None, :]
    share = jnp.sum(jnp.where(named, weights[:, :, None], 0.0), axis=1)
    high = lax.reduce_precision(share, 8, 7)
    middle = lax.reduce_precision(share - high, 8, 7)
    low = share - high - middle
    pieces = jnp.concatenate([high, middle, low], axis=1)
    pieces = jnp.pad(pieces, ((0, 0), (0, LANES - 3 * experts)))
    return pieces.astype(jnp.bfloat16)


def per_device(tokens, router_logits, expert_ids, w_gate, w_up, w_down):
    chips = lax.axis_size(("exp", "tp"))
    experts = lax.axis_size(("sect", "exp")) // 4
    bits = chips.bit_length() - 1
    model_width = tokens.shape[1]
    chunk_width = model_width // CHUNKS

    def swap_with(flips):
        return [
            (core * chips + chip, (core ^ flips[2]) * chips + (chip ^ flips[core]))
            for core in range(2)
            for chip in range(chips)
        ]

    high_bits = list(range(bits - 1, 1, -1))
    orders = (high_bits + [1, 0], high_bits + [0, 1])
    chip_swaps = [swap_with((1 << a, 1 << b, 0)) for a, b in zip(*orders)]
    core_swap = swap_with((0, 0, 1))

    my_expert = lax.axis_index(("sect", "exp")) // 4
    lane = jnp.arange(LANES, dtype=jnp.int32)[None, :]
    pick = jnp.where((lane % experts == my_expert) & (lane < 3 * experts), 1.0, 0.0)

    prev = ()
    for chunk in range(CHUNKS):
        rows = tokens[:, chunk * chunk_width : (chunk + 1) * chunk_width]
        last = chunk == CHUNKS - 1
        if last:
            shares = share_columns(router_logits, expert_ids, experts)
            rows = jnp.concatenate([rows, shares], axis=1)
        for pairs in chip_swaps:
            rows = jnp.concatenate([rows, lax.ppermute(rows, AXES, pairs)], axis=0)
        other = lax.ppermute(rows, AXES, core_swap)
        prev = gate_up((rows, other), w_gate, w_up, chunk, chunk_width, prev, last)
    hidden = prev[0]

    results = []
    for chunk in range(CHUNKS):
        keep, send = down(pick, hidden, w_down, rows, other, chunk, chunk_width)
        total = keep + lax.ppermute(send, AXES, core_swap).astype(jnp.float32)
        for pairs in chip_swaps[::-1]:
            half = total.shape[0] // 2
            send = total[half:].astype(jnp.bfloat16)
            received = lax.ppermute(send, AXES, pairs)
            total = total[:half] + received.astype(jnp.float32)
        results.append(total.astype(jnp.bfloat16))
    return jnp.concatenate(results, axis=1)


def solution(mesh):
    in_specs = (
        P(AXES, None),
        P(AXES, None),
        P(AXES, None),
        P(("sect", "exp"), None, "tp"),
        P(("sect", "exp"), None, "tp"),
        P(("sect", "exp"), "tp", None),
    )
    return jax.shard_map(
        per_device, mesh=mesh, in_specs=in_specs, out_specs=P(AXES, None), check_vma=False
    )
```

```python
import jax
import jax.numpy as jnp
from jax import lax
from jax.experimental import pallas as pl
from jax.experimental.pallas import tpu as pltpu
from jax.sharding import PartitionSpec as P

AXES = ("sect", "exp", "tp")
LANES = 128
TILE = 256
SCOPED = 1 << 20
SMALL = 2 << 20
GIGA = 10**9
STACK_COST = ((1, 1), (4, 4))
FFN_COST = (0.1, 0.1, 0.1, 0.1, 0.1)
STRIP = 512
VMEM = pl.BlockSpec(memory_space=pltpu.VMEM)
ANY = pl.BlockSpec(memory_space=pl.ANY)
HBM = pl.BlockSpec(memory_space=pltpu.HBM)


def side_by_side(parts, depth):
    return jnp.concatenate([p[:, :depth] for p in parts], axis=0)


def pair_kernel(depth, part_count, *refs):
    parts, (wg_ref, wu_ref) = refs[:part_count], refs[part_count : part_count + 2]
    gate_ref, up_ref = refs[-2:]
    for at in range(0, gate_ref.shape[1], TILE):
        columns = pl.ds(at, TILE)
        rows = side_by_side(parts, depth)
        for w_ref, out_ref in ((wg_ref, gate_ref), (wu_ref, up_ref)):
            out_ref[:, columns] = jnp.dot(
                rows, w_ref[0, :depth, columns], preferred_element_type=jnp.float32
            )


def pair(parts, w_gate, w_up, depth, cost, after=()):
    row_count = sum(p.shape[0] for p in parts)
    width = w_gate.shape[2]
    return pl.pallas_call(
        lambda *refs: pair_kernel(depth, len(parts), *refs),
        in_specs=[VMEM] * (len(parts) + 2) + [ANY] * len(after),
        out_specs=[VMEM] * 2,
        out_shape=[jax.ShapeDtypeStruct((row_count, width), jnp.float32)] * 2,
        cost_estimate=pl.CostEstimate(flops=int(cost * GIGA), bytes_accessed=0, transcendentals=0),
        compiler_params=pltpu.CompilerParams(vmem_limit_bytes=SCOPED),
        name="pair",
    )(*parts, w_gate, w_up, *after)


def hidden_kernel(depth, part_count, *refs):
    parts, refs = refs[:part_count], refs[part_count:]
    weights, sums, hidden_ref = refs[:2], refs[2:4], refs[-1]
    for at in range(0, hidden_ref.shape[1], TILE):
        columns = pl.ds(at, TILE)
        rows = side_by_side(parts, depth)
        gate, up = [
            total[:, columns]
            + jnp.dot(
                rows, weight[0, pl.ds(depth, depth), columns], preferred_element_type=jnp.float32
            )
            for weight, total in zip(weights, sums)
        ]
        hidden_ref[:, columns] = (gate / (1.0 + jnp.exp(-gate)) * up).astype(jnp.bfloat16)


def hidden_rows(parts, w_gate, w_up, sums, depth, cost, after=()):
    row_count = sum(p.shape[0] for p in parts)
    width = w_gate.shape[2]
    return pl.pallas_call(
        lambda *refs: hidden_kernel(depth, len(parts), *refs),
        in_specs=[VMEM] * (len(parts) + 2 + len(sums)) + [ANY] * len(after),
        out_specs=VMEM,
        out_shape=jax.ShapeDtypeStruct((row_count, width), jnp.bfloat16),
        cost_estimate=pl.CostEstimate(
            flops=int(cost * GIGA), bytes_accessed=0, transcendentals=row_count * width
        ),
        compiler_params=pltpu.CompilerParams(vmem_limit_bytes=SCOPED),
        name="hidden_rows",
    )(*parts, w_gate, w_up, *sums, *after)


def down_kernel(first, experts, group_count, *refs):
    hidden, wd_ref, parts = refs[:group_count], refs[group_count], refs[group_count + 1 : -2]
    keep_ref, send_ref = refs[-2:]
    quarter = parts[0].shape[0]
    entry = lax.axis_index("sect") * lax.axis_size("exp") + lax.axis_index("exp")

    def share(part):
        lanes = part.shape[1] - LANES
        lane = lax.broadcasted_iota(jnp.int32, (quarter, LANES), 1)
        chosen = (lane % experts == entry // 4) & (lane < 3 * experts)
        shares = jnp.where(chosen, part[:, lanes:].astype(jnp.float32), 0.0)
        return jnp.sum(shares, axis=1, keepdims=True)

    shares = [share(p) for p in parts]
    for at in range(0, keep_ref.shape[1], TILE):
        columns = pl.ds(at, TILE)
        rows = jnp.concatenate([h[...] for h in hidden], axis=0)
        out = jnp.dot(
            rows, wd_ref[0, :, pl.ds(first + at, TILE)], preferred_element_type=jnp.float32
        )
        for k, part_share in enumerate(shares):
            piece = part_share * out[k * quarter : (k + 1) * quarter]
            place = pl.ds(k // 2 * quarter, quarter)
            if k % 2 == 0:
                keep_ref[place, columns] = piece
            else:
                send_ref[place, columns] = piece.astype(jnp.bfloat16)


def down(experts, hidden, w_down, parts, chunk, chunk_width, cost):
    half = sum(h.shape[0] for h in hidden) // 2
    first = chunk * chunk_width
    return pl.pallas_call(
        lambda *refs: down_kernel(first, experts, len(hidden), *refs),
        in_specs=[VMEM] * (len(hidden) + 1 + len(parts)),
        out_specs=[VMEM] * 2,
        out_shape=[
            jax.ShapeDtypeStruct((half, chunk_width), jnp.float32),
            jax.ShapeDtypeStruct((half, chunk_width), jnp.bfloat16),
        ],
        cost_estimate=pl.CostEstimate(
            flops=int(cost * GIGA), bytes_accessed=0, transcendentals=0
        ),
        compiler_params=pltpu.CompilerParams(vmem_limit_bytes=SCOPED),
        name="down",
    )(*hidden, w_down, *parts)


def small_call(kernel, name, out_shape, *operands, after=(), flops=10**6):
    return pl.pallas_call(
        kernel,
        in_specs=[VMEM] * len(operands) + [ANY] * len(after),
        out_specs=jax.tree.map(lambda _: VMEM, out_shape),
        out_shape=out_shape,
        cost_estimate=pl.CostEstimate(flops=flops, bytes_accessed=0, transcendentals=0),
        compiler_params=pltpu.CompilerParams(vmem_limit_bytes=SMALL),
        name=name,
    )(*operands, *after)


def cut_kernel(experts, tokens_hbm, logits_hbm, ids_hbm, plain_ref, shared_ref, *scratch):
    tokens_ref, logits_ref, ids_ref, sems = scratch
    sources = (tokens_hbm, logits_hbm, ids_hbm)
    copies = [
        pltpu.make_async_copy(src, dst, sems.at[k])
        for k, (src, dst) in enumerate(zip(sources, scratch))
    ]
    for copy in copies:
        copy.start()
    for copy in copies:
        copy.wait()
    row_count, width = plain_ref.shape
    plain_ref[...] = tokens_ref[:, :width]
    shared_ref[:, :width] = tokens_ref[:, width:]
    square = (row_count, row_count)
    diagonal = lax.broadcasted_iota(jnp.int32, square, 0) == lax.broadcasted_iota(
        jnp.int32, square, 1
    )

    def column(row):
        spread = jnp.broadcast_to(row, square)
        return jnp.sum(jnp.where(diagonal, spread, 0.0), axis=1, keepdims=True)

    logits = [column(logits_ref[k : k + 1, :]) for k in range(2)]
    ids = [column(ids_ref[k : k + 1, :].astype(jnp.float32)) for k in range(2)]
    lane = lax.broadcasted_iota(jnp.int32, (row_count, LANES), 1)
    expert = (lane % experts).astype(jnp.float32)
    share = jnp.zeros((row_count, LANES), jnp.float32)
    for k in range(2):
        prob = 1.0 / (1.0 + jnp.exp(logits[1 - k] - logits[k]))
        share = share + jnp.where(ids[k] == expert, prob, 0.0)
    high = share.astype(jnp.bfloat16).astype(jnp.float32)
    middle = (share - high).astype(jnp.bfloat16).astype(jnp.float32)
    low = share - high - middle
    piece = lane // experts
    pieces = jnp.where(piece == 0, high, jnp.where(piece == 1, middle, low))
    shared_ref[:, width:] = jnp.where(piece < 3, pieces, 0.0).astype(jnp.bfloat16)


def stack_kernel(fan, *refs):
    out_ref = refs[-1]
    count = refs[0].shape[0]
    if count % 16:
        blocks = [r[...].astype(jnp.float32) for r in refs[:fan]]
        out_ref[...] = jnp.concatenate(blocks, axis=0).astype(out_ref.dtype)
    else:
        for k in range(fan):
            out_ref[k * count : (k + 1) * count] = refs[k][...]


def stack(mine, received, after, flops):
    fan = 1 + len(received)
    return small_call(
        lambda *refs: stack_kernel(fan, *refs),
        "stack",
        jax.ShapeDtypeStruct((fan * mine.shape[0], mine.shape[1]), mine.dtype),
        mine,
        *received,
        after=after,
        flops=flops,
    )


def merge_kernel(taken, fan, total_ref, *refs):
    received, (keep_ref, *sent) = refs[:taken], refs[len(refs) - fan :]
    count = keep_ref.shape[0]
    for at in range(0, total_ref.shape[1], STRIP):
        columns = pl.ds(at, STRIP)
        total = total_ref[:, columns]
        for r in received:
            total = total + r[:, columns].astype(jnp.float32)
        keep_ref[:, columns] = total[:count]
        for k in range(1, fan):
            piece = total[k * count : (k + 1) * count]
            sent[k - 1][:, columns] = piece.astype(jnp.bfloat16)


def merge(total, received, fan, after):
    shape = (total.shape[0] // fan, total.shape[1])
    keep, *sent = small_call(
        lambda *refs: merge_kernel(len(received), fan, *refs),
        "merge",
        [jax.ShapeDtypeStruct(shape, jnp.float32 if k == 0 else jnp.bfloat16) for k in range(fan)],
        total,
        *received,
        after=after,
    )
    return keep, sent


def finish_kernel(taken, *refs):
    out_ref = refs[-1]
    at = 0
    for k in range(2):
        total_ref, *received = refs[k * (taken + 1) : (k + 1) * (taken + 1)]
        columns = pl.ds(at, total_ref.shape[1])
        total = total_ref[...]
        for r in received:
            total = total + r[...].astype(jnp.float32)
        out_ref[:, columns] = total.astype(jnp.bfloat16)
        at += total_ref.shape[1]


def per_device(tokens, router_logits, expert_ids, w_gate, w_up, w_down):
    chips = lax.axis_size(("exp", "tp"))
    experts = lax.axis_size(("sect", "exp")) // 4
    bits = chips.bit_length() - 1
    own, model_width = tokens.shape
    width = model_width // 2

    def swap_with(flips):
        return [
            (core * chips + chip, (core ^ flips[2]) * chips + (chip ^ flips[core]))
            for core in range(2)
            for chip in range(chips)
        ]

    def permute(rows, step):
        rows = rows if isinstance(rows, list) else [rows] * len(step)
        return [lax.ppermute(r, AXES, swap_with(flips)) for r, flips in zip(rows, step)]

    core_swap = [(0, 0, 1)]
    steps = [[(1 << k, 1 << k, 0)] for k in range(bits - 1, 3, -1)]
    steps.append([(m, m, 0) for m in (4, 8, 12)])
    steps.append([(2, 1, 0)])
    steps.append([(1, 2, 0)])

    sources = [
        pltpu.with_memory_space_constraint(x, pltpu.HBM)
        for x in (tokens, router_logits.T, expert_ids.T)
    ]
    rows = pl.pallas_call(
        lambda *refs: cut_kernel(experts, *refs),
        in_specs=[HBM] * 3,
        out_specs=[VMEM] * 2,
        out_shape=[
            jax.ShapeDtypeStruct((own, width), tokens.dtype),
            jax.ShapeDtypeStruct((own, width + LANES), tokens.dtype),
        ],
        scratch_shapes=[pltpu.VMEM(x.shape, x.dtype) for x in sources]
        + [pltpu.SemaphoreType.DMA((3,))],
        cost_estimate=pl.CostEstimate(flops=10**6, bytes_accessed=0, transcendentals=0),
        compiler_params=pltpu.CompilerParams(vmem_limit_bytes=2 << 20),
        name="cut",
    )(*sources)
    rows = list(rows)
    flying = [permute(r, steps[0]) for r in rows]
    for k in range(len(steps) - 1):
        for c in range(2):
            rows[c] = stack(rows[c], flying[c], (rows[1 - c],), int(STACK_COST[c][min(k, 1)] * GIGA))
            flying[c] = permute(rows[c], steps[k + 1])
    early = [permute(r, core_swap)[0] for r in rows]
    arrived = [f[0] for f in flying]
    weights, cost = (w_gate, w_up), FFN_COST

    sums = list(pair((rows[0], early[0]), *weights, width, cost[0], (rows[1],)))
    arrived[0], sums[0] = lax.optimization_barrier((arrived[0], sums[0]))
    late = permute(arrived[0], core_swap)[0]
    hidden = [hidden_rows((rows[1], early[1]), *weights, sums, width, cost[1], (arrived[0],))]
    sums = list(pair((arrived[0], late), *weights, width, cost[2], (hidden[0],)))
    arrived[1], sums[0] = lax.optimization_barrier((arrived[1], sums[0]))
    late = permute(arrived[1], core_swap)[0]
    hidden.append(hidden_rows((arrived[1], late), *weights, sums, width, cost[3]))
    parts = (rows[1], early[1], arrived[1], late)

    totals, flying = [], []
    for c in range(2):
        kept, sent = down(experts, hidden, w_down, parts, c, width, cost[4])
        totals.append(kept)
        flying.append(permute([sent], core_swap))
    for step in steps[::-1]:
        for c in range(2):
            totals[c], sent = merge(totals[c], flying[c], 1 + len(step), (totals[1 - c],))
            flying[c] = permute(sent, step)
    return small_call(
        lambda *refs: finish_kernel(len(flying[0]), *refs),
        "finish",
        jax.ShapeDtypeStruct(tokens.shape, tokens.dtype),
        totals[0],
        *flying[0],
        totals[1],
        *flying[1],
    )


def solution(mesh):
    in_specs = (
        P(AXES, None),
        P(AXES, None),
        P(AXES, None),
        P(("sect", "exp"), None, "tp"),
        P(("sect", "exp"), None, "tp"),
        P(("sect", "exp"), "tp", None),
    )
    return jax.shard_map(
        per_device, mesh=mesh, in_specs=in_specs, out_specs=P(AXES, None), check_vma=False
    )
```

```python
import jax
import jax.numpy as jnp
from jax import lax
from jax.experimental import pallas as pl
from jax.experimental.pallas import tpu as pltpu
from jax.sharding import PartitionSpec as P

AXES = ("sect", "exp", "tp")
LANES = 128
TILE = 256
SCOPED = 1 << 20
SMALL = 2 << 20
GIGA = 10**9
STACK_COST = ((1, 1), (4, 4))
FFN_COST = (0.1, 0.1, 0.1, 0.1, 0.1)
STRIP = 512
VMEM = pl.BlockSpec(memory_space=pltpu.VMEM)
ANY = pl.BlockSpec(memory_space=pl.ANY)
HBM = pl.BlockSpec(memory_space=pltpu.HBM)


def side_by_side(parts, depth):
    return jnp.concatenate([p[:, :depth] for p in parts], axis=0)


def pair_kernel(depth, part_count, *refs):
    parts, (wg_ref, wu_ref) = refs[:part_count], refs[part_count : part_count + 2]
    gate_ref, up_ref = refs[-2:]
    for at in range(0, gate_ref.shape[1], TILE):
        columns = pl.ds(at, TILE)
        rows = side_by_side(parts, depth)
        for w_ref, out_ref in ((wg_ref, gate_ref), (wu_ref, up_ref)):
            out_ref[:, columns] = jnp.dot(
                rows, w_ref[0, :depth, columns], preferred_element_type=jnp.float32
            )


def pair(parts, w_gate, w_up, depth, cost, after=()):
    row_count = sum(p.shape[0] for p in parts)
    width = w_gate.shape[2]
    return pl.pallas_call(
        lambda *refs: pair_kernel(depth, len(parts), *refs),
        in_specs=[VMEM] * (len(parts) + 2) + [ANY] * len(after),
        out_specs=[VMEM] * 2,
        out_shape=[jax.ShapeDtypeStruct((row_count, width), jnp.float32)] * 2,
        cost_estimate=pl.CostEstimate(flops=int(cost * GIGA), bytes_accessed=0, transcendentals=0),
        compiler_params=pltpu.CompilerParams(vmem_limit_bytes=SCOPED),
        name="pair",
    )(*parts, w_gate, w_up, *after)


def hidden_kernel(depth, part_count, *refs):
    parts, refs = refs[:part_count], refs[part_count:]
    weights, sums, hidden_ref = refs[:2], refs[2:4], refs[-1]
    for at in range(0, hidden_ref.shape[1], TILE):
        columns = pl.ds(at, TILE)
        rows = side_by_side(parts, depth)
        gate, up = [
            total[:, columns]
            + jnp.dot(
                rows, weight[0, pl.ds(depth, depth), columns], preferred_element_type=jnp.float32
            )
            for weight, total in zip(weights, sums)
        ]
        hidden_ref[:, columns] = (gate / (1.0 + jnp.exp(-gate)) * up).astype(jnp.bfloat16)


def hidden_rows(parts, w_gate, w_up, sums, depth, cost, after=()):
    row_count = sum(p.shape[0] for p in parts)
    width = w_gate.shape[2]
    return pl.pallas_call(
        lambda *refs: hidden_kernel(depth, len(parts), *refs),
        in_specs=[VMEM] * (len(parts) + 2 + len(sums)) + [ANY] * len(after),
        out_specs=VMEM,
        out_shape=jax.ShapeDtypeStruct((row_count, width), jnp.bfloat16),
        cost_estimate=pl.CostEstimate(
            flops=int(cost * GIGA), bytes_accessed=0, transcendentals=row_count * width
        ),
        compiler_params=pltpu.CompilerParams(vmem_limit_bytes=SCOPED),
        name="hidden_rows",
    )(*parts, w_gate, w_up, *sums, *after)


def down_kernel(first, experts, group_count, *refs):
    hidden, wd_ref, parts = refs[:group_count], refs[group_count], refs[group_count + 1 : -2]
    keep_ref, send_ref = refs[-2:]
    quarter = parts[0].shape[0]
    entry = lax.axis_index("sect") * lax.axis_size("exp") + lax.axis_index("exp")

    def share(part):
        lanes = part.shape[1] - LANES
        lane = lax.broadcasted_iota(jnp.int32, (quarter, LANES), 1)
        chosen = (lane % experts == entry // 4) & (lane < 3 * experts)
        shares = jnp.where(chosen, part[:, lanes:].astype(jnp.float32), 0.0)
        return jnp.sum(shares, axis=1, keepdims=True)

    shares = [share(p) for p in parts]
    for at in range(0, keep_ref.shape[1], TILE):
        columns = pl.ds(at, TILE)
        rows = jnp.concatenate([h[...] for h in hidden], axis=0)
        out = jnp.dot(
            rows, wd_ref[0, :, pl.ds(first + at, TILE)], preferred_element_type=jnp.float32
        )
        for k, part_share in enumerate(shares):
            piece = part_share * out[k * quarter : (k + 1) * quarter]
            place = pl.ds(k // 2 * quarter, quarter)
            if k % 2 == 0:
                keep_ref[place, columns] = piece
            else:
                send_ref[place, columns] = piece.astype(jnp.bfloat16)


def down(experts, hidden, w_down, parts, chunk, chunk_width, cost):
    half = sum(h.shape[0] for h in hidden) // 2
    first = chunk * chunk_width
    return pl.pallas_call(
        lambda *refs: down_kernel(first, experts, len(hidden), *refs),
        in_specs=[VMEM] * (len(hidden) + 1 + len(parts)),
        out_specs=[VMEM] * 2,
        out_shape=[
            jax.ShapeDtypeStruct((half, chunk_width), jnp.float32),
            jax.ShapeDtypeStruct((half, chunk_width), jnp.bfloat16),
        ],
        cost_estimate=pl.CostEstimate(
            flops=int(cost * GIGA), bytes_accessed=0, transcendentals=0
        ),
        compiler_params=pltpu.CompilerParams(vmem_limit_bytes=SCOPED),
        name="down",
    )(*hidden, w_down, *parts)


def small_call(kernel, name, out_shape, *operands, after=(), flops=10**6):
    return pl.pallas_call(
        kernel,
        in_specs=[VMEM] * len(operands) + [ANY] * len(after),
        out_specs=jax.tree.map(lambda _: VMEM, out_shape),
        out_shape=out_shape,
        cost_estimate=pl.CostEstimate(flops=flops, bytes_accessed=0, transcendentals=0),
        compiler_params=pltpu.CompilerParams(vmem_limit_bytes=SMALL),
        name=name,
    )(*operands, *after)


def cut_kernel(experts, tokens_hbm, logits_hbm, ids_hbm, plain_ref, shared_ref, *scratch):
    tokens_ref, logits_ref, ids_ref, sems = scratch
    sources = (tokens_hbm, logits_hbm, ids_hbm)
    copies = [
        pltpu.make_async_copy(src, dst, sems.at[k])
        for k, (src, dst) in enumerate(zip(sources, scratch))
    ]
    for copy in copies:
        copy.start()
    for copy in copies:
        copy.wait()
    row_count, width = plain_ref.shape
    plain_ref[...] = tokens_ref[:, :width]
    shared_ref[:, :width] = tokens_ref[:, width:]
    square = (row_count, row_count)
    diagonal = lax.broadcasted_iota(jnp.int32, square, 0) == lax.broadcasted_iota(
        jnp.int32, square, 1
    )

    def column(row):
        spread = jnp.broadcast_to(row, square)
        return jnp.sum(jnp.where(diagonal, spread, 0.0), axis=1, keepdims=True)

    logits = [column(logits_ref[k : k + 1, :]) for k in range(2)]
    ids = [column(ids_ref[k : k + 1, :].astype(jnp.float32)) for k in range(2)]
    lane = lax.broadcasted_iota(jnp.int32, (row_count, LANES), 1)
    expert = (lane % experts).astype(jnp.float32)
    share = jnp.zeros((row_count, LANES), jnp.float32)
    for k in range(2):
        prob = 1.0 / (1.0 + jnp.exp(logits[1 - k] - logits[k]))
        share = share + jnp.where(ids[k] == expert, prob, 0.0)
    high = share.astype(jnp.bfloat16).astype(jnp.float32)
    middle = (share - high).astype(jnp.bfloat16).astype(jnp.float32)
    low = share - high - middle
    piece = lane // experts
    pieces = jnp.where(piece == 0, high, jnp.where(piece == 1, middle, low))
    shared_ref[:, width:] = jnp.where(piece < 3, pieces, 0.0).astype(jnp.bfloat16)


def stack_kernel(fan, *refs):
    out_ref = refs[-1]
    count = refs[0].shape[0]
    if count % 16:
        blocks = [r[...].astype(jnp.float32) for r in refs[:fan]]
        out_ref[...] = jnp.concatenate(blocks, axis=0).astype(out_ref.dtype)
    else:
        for k in range(fan):
            out_ref[k * count : (k + 1) * count] = refs[k][...]


def stack(mine, received, after, flops):
    fan = 1 + len(received)
    return small_call(
        lambda *refs: stack_kernel(fan, *refs),
        "stack",
        jax.ShapeDtypeStruct((fan * mine.shape[0], mine.shape[1]), mine.dtype),
        mine,
        *received,
        after=after,
        flops=flops,
    )


def merge_kernel(taken, fan, total_ref, *refs):
    received, (keep_ref, *sent) = refs[:taken], refs[len(refs) - fan :]
    count = keep_ref.shape[0]
    for at in range(0, total_ref.shape[1], STRIP):
        columns = pl.ds(at, STRIP)
        total = total_ref[:, columns]
        for r in received:
            total = total + r[:, columns].astype(jnp.float32)
        keep_ref[:, columns] = total[:count]
        for k in range(1, fan):
            piece = total[k * count : (k + 1) * count]
            sent[k - 1][:, columns] = piece.astype(jnp.bfloat16)


def merge(total, received, fan, after):
    shape = (total.shape[0] // fan, total.shape[1])
    keep, *sent = small_call(
        lambda *refs: merge_kernel(len(received), fan, *refs),
        "merge",
        [jax.ShapeDtypeStruct(shape, jnp.float32 if k == 0 else jnp.bfloat16) for k in range(fan)],
        total,
        *received,
        after=after,
    )
    return keep, sent


def finish_kernel(taken, *refs):
    out_ref = refs[-1]
    at = 0
    for k in range(2):
        total_ref, *received = refs[k * (taken + 1) : (k + 1) * (taken + 1)]
        columns = pl.ds(at, total_ref.shape[1])
        total = total_ref[...]
        for r in received:
            total = total + r[...].astype(jnp.float32)
        out_ref[:, columns] = total.astype(jnp.bfloat16)
        at += total_ref.shape[1]


def per_device(tokens, router_logits, expert_ids, w_gate, w_up, w_down):
    chips = lax.axis_size(("exp", "tp"))
    experts = lax.axis_size(("sect", "exp")) // 4
    bits = chips.bit_length() - 1
    own, model_width = tokens.shape
    width = model_width // 2

    def swap_with(flips):
        return [
            (core * chips + chip, (core ^ flips[2]) * chips + (chip ^ flips[core]))
            for core in range(2)
            for chip in range(chips)
        ]

    def permute(rows, step):
        rows = rows if isinstance(rows, list) else [rows] * len(step)
        return [lax.ppermute(r, AXES, swap_with(flips)) for r, flips in zip(rows, step)]

    core_swap = [(0, 0, 1)]
    steps = [[(1 << k, 1 << k, 0)] for k in range(bits - 1, 3, -1)]
    steps.append([(m, m, 0) for m in (4, 8, 12)])
    steps.append([(2, 1, 0)])
    steps.append([(1, 2, 0)])

    sources = [
        pltpu.with_memory_space_constraint(x, pltpu.HBM)
        for x in (tokens, router_logits.T, expert_ids.T)
    ]
    rows = pl.pallas_call(
        lambda *refs: cut_kernel(experts, *refs),
        in_specs=[HBM] * 3,
        out_specs=[VMEM] * 2,
        out_shape=[
            jax.ShapeDtypeStruct((own, width), tokens.dtype),
            jax.ShapeDtypeStruct((own, width + LANES), tokens.dtype),
        ],
        scratch_shapes=[pltpu.VMEM(x.shape, x.dtype) for x in sources]
        + [pltpu.SemaphoreType.DMA((3,))],
        cost_estimate=pl.CostEstimate(flops=10**6, bytes_accessed=0, transcendentals=0),
        compiler_params=pltpu.CompilerParams(vmem_limit_bytes=2 << 20),
        name="cut",
    )(*sources)
    rows = list(rows)
    flying = [permute(r, steps[0]) for r in rows]
    for k in range(len(steps) - 1):
        for c in range(2):
            rows[c] = stack(rows[c], flying[c], (rows[1 - c],), int(STACK_COST[c][min(k, 1)] * GIGA))
            flying[c] = permute(rows[c], steps[k + 1])
    early = [permute(r, core_swap)[0] for r in rows]
    arrived = [f[0] for f in flying]
    weights, cost = (w_gate, w_up), FFN_COST

    sums = list(pair((rows[0], early[0]), *weights, width, cost[0], (rows[1],)))
    arrived[0], sums[0] = lax.optimization_barrier((arrived[0], sums[0]))
    late = permute(arrived[0], core_swap)[0]
    hidden = [hidden_rows((rows[1], early[1]), *weights, sums, width, cost[1], (arrived[0],))]
    sums = list(pair((arrived[0], late), *weights, width, cost[2], (hidden[0],)))
    arrived[1], sums[0] = lax.optimization_barrier((arrived[1], sums[0]))
    late = permute(arrived[1], core_swap)[0]
    hidden.append(hidden_rows((arrived[1], late), *weights, sums, width, cost[3]))
    parts = (rows[1], early[1], arrived[1], late)

    totals, flying = [], []
    for c in range(2):
        kept, sent = down(experts, hidden, w_down, parts, c, width, cost[4])
        totals.append(kept)
        flying.append(permute([sent], core_swap))
    for step in steps[::-1]:
        for c in range(2):
            totals[c], sent = merge(totals[c], flying[c], 1 + len(step), (totals[1 - c],))
            flying[c] = permute(sent, step)
    return small_call(
        lambda *refs: finish_kernel(len(flying[0]), *refs),
        "finish",
        jax.ShapeDtypeStruct(tokens.shape, tokens.dtype),
        totals[0],
        *flying[0][::-1],
        totals[1],
        *flying[1][::-1],
    )


def solution(mesh):
    in_specs = (
        P(AXES, None),
        P(AXES, None),
        P(AXES, None),
        P(("sect", "exp"), None, "tp"),
        P(("sect", "exp"), None, "tp"),
        P(("sect", "exp"), "tp", None),
    )
    return jax.shard_map(
        per_device, mesh=mesh, in_specs=in_specs, out_specs=P(AXES, None), check_vma=False
    )
```

```python
import jax
import jax.numpy as jnp
from jax import lax
from jax.experimental import pallas as pl
from jax.experimental.pallas import tpu as pltpu
from jax.sharding import PartitionSpec as P

AXES = ("sect", "exp", "tp")
LANES = 128
TILE = 256
SCOPED = 1 << 20
SMALL = 2 << 20
GIGA = 10**9
MERGE_COST = (0.001, 0.001, 0.001)
STACK_COST = ((1, 1), (4, 4))
FFN_COST = (0.1, 0.1, 0.1, 0.1, 0.1)
STRIP = 512
VMEM = pl.BlockSpec(memory_space=pltpu.VMEM)
ANY = pl.BlockSpec(memory_space=pl.ANY)
HBM = pl.BlockSpec(memory_space=pltpu.HBM)


def side_by_side(parts, depth):
    return jnp.concatenate([p[:, :depth] for p in parts], axis=0)


def pair_kernel(depth, part_count, *refs):
    parts, (wg_ref, wu_ref) = refs[:part_count], refs[part_count : part_count + 2]
    gate_ref, up_ref = refs[-2:]
    for at in range(0, gate_ref.shape[1], TILE):
        columns = pl.ds(at, TILE)
        rows = side_by_side(parts, depth)
        for w_ref, out_ref in ((wg_ref, gate_ref), (wu_ref, up_ref)):
            out_ref[:, columns] = jnp.dot(
                rows, w_ref[0, :depth, columns], preferred_element_type=jnp.float32
            )


def pair(parts, w_gate, w_up, depth, cost, after=()):
    row_count = sum(p.shape[0] for p in parts)
    width = w_gate.shape[2]
    return pl.pallas_call(
        lambda *refs: pair_kernel(depth, len(parts), *refs),
        in_specs=[VMEM] * (len(parts) + 2) + [ANY] * len(after),
        out_specs=[VMEM] * 2,
        out_shape=[jax.ShapeDtypeStruct((row_count, width), jnp.float32)] * 2,
        cost_estimate=pl.CostEstimate(flops=int(cost * GIGA), bytes_accessed=0, transcendentals=0),
        compiler_params=pltpu.CompilerParams(vmem_limit_bytes=SCOPED),
        name="pair",
    )(*parts, w_gate, w_up, *after)


def hidden_kernel(depth, part_count, *refs):
    parts, refs = refs[:part_count], refs[part_count:]
    weights, sums, hidden_ref = refs[:2], refs[2:4], refs[-1]
    for at in range(0, hidden_ref.shape[1], TILE):
        columns = pl.ds(at, TILE)
        rows = side_by_side(parts, depth)
        gate, up = [
            total[:, columns]
            + jnp.dot(
                rows, weight[0, pl.ds(depth, depth), columns], preferred_element_type=jnp.float32
            )
            for weight, total in zip(weights, sums)
        ]
        hidden_ref[:, columns] = (gate / (1.0 + jnp.exp(-gate)) * up).astype(jnp.bfloat16)


def hidden_rows(parts, w_gate, w_up, sums, depth, cost, after=()):
    row_count = sum(p.shape[0] for p in parts)
    width = w_gate.shape[2]
    return pl.pallas_call(
        lambda *refs: hidden_kernel(depth, len(parts), *refs),
        in_specs=[VMEM] * (len(parts) + 2 + len(sums)) + [ANY] * len(after),
        out_specs=VMEM,
        out_shape=jax.ShapeDtypeStruct((row_count, width), jnp.bfloat16),
        cost_estimate=pl.CostEstimate(
            flops=int(cost * GIGA), bytes_accessed=0, transcendentals=row_count * width
        ),
        compiler_params=pltpu.CompilerParams(vmem_limit_bytes=SCOPED),
        name="hidden_rows",
    )(*parts, w_gate, w_up, *sums, *after)


def down_kernel(first, experts, group_count, *refs):
    hidden, wd_ref, parts = refs[:group_count], refs[group_count], refs[group_count + 1 : -2]
    keep_ref, send_ref = refs[-2:]
    quarter = parts[0].shape[0]
    entry = lax.axis_index("sect") * lax.axis_size("exp") + lax.axis_index("exp")

    def share(part):
        lanes = part.shape[1] - LANES
        lane = lax.broadcasted_iota(jnp.int32, (quarter, LANES), 1)
        chosen = (lane % experts == entry // 4) & (lane < 3 * experts)
        shares = jnp.where(chosen, part[:, lanes:].astype(jnp.float32), 0.0)
        return jnp.sum(shares, axis=1, keepdims=True)

    shares = [share(p) for p in parts]
    for at in range(0, keep_ref.shape[1], TILE):
        columns = pl.ds(at, TILE)
        rows = jnp.concatenate([h[...] for h in hidden], axis=0)
        out = jnp.dot(
            rows, wd_ref[0, :, pl.ds(first + at, TILE)], preferred_element_type=jnp.float32
        )
        for k, part_share in enumerate(shares):
            piece = part_share * out[k * quarter : (k + 1) * quarter]
            place = pl.ds(k // 2 * quarter, quarter)
            if k % 2 == 0:
                keep_ref[place, columns] = piece
            else:
                send_ref[place, columns] = piece.astype(jnp.bfloat16)


def down(experts, hidden, w_down, parts, chunk, chunk_width, cost):
    half = sum(h.shape[0] for h in hidden) // 2
    first = chunk * chunk_width
    return pl.pallas_call(
        lambda *refs: down_kernel(first, experts, len(hidden), *refs),
        in_specs=[VMEM] * (len(hidden) + 1 + len(parts)),
        out_specs=[VMEM] * 2,
        out_shape=[
            jax.ShapeDtypeStruct((half, chunk_width), jnp.float32),
            jax.ShapeDtypeStruct((half, chunk_width), jnp.bfloat16),
        ],
        cost_estimate=pl.CostEstimate(
            flops=int(cost * GIGA), bytes_accessed=0, transcendentals=0
        ),
        compiler_params=pltpu.CompilerParams(vmem_limit_bytes=SCOPED),
        name="down",
    )(*hidden, w_down, *parts)


def small_call(kernel, name, out_shape, *operands, after=(), flops=10**6):
    return pl.pallas_call(
        kernel,
        in_specs=[VMEM] * len(operands) + [ANY] * len(after),
        out_specs=jax.tree.map(lambda _: VMEM, out_shape),
        out_shape=out_shape,
        cost_estimate=pl.CostEstimate(flops=flops, bytes_accessed=0, transcendentals=0),
        compiler_params=pltpu.CompilerParams(vmem_limit_bytes=SMALL),
        name=name,
    )(*operands, *after)


def cut_kernel(experts, tokens_hbm, logits_hbm, ids_hbm, plain_ref, shared_ref, *scratch):
    tokens_ref, logits_ref, ids_ref, sems = scratch
    sources = (tokens_hbm, logits_hbm, ids_hbm)
    copies = [
        pltpu.make_async_copy(src, dst, sems.at[k])
        for k, (src, dst) in enumerate(zip(sources, scratch))
    ]
    for copy in copies:
        copy.start()
    for copy in copies:
        copy.wait()
    row_count, width = plain_ref.shape
    plain_ref[...] = tokens_ref[:, :width]
    shared_ref[:, :width] = tokens_ref[:, width:]
    square = (row_count, row_count)
    diagonal = lax.broadcasted_iota(jnp.int32, square, 0) == lax.broadcasted_iota(
        jnp.int32, square, 1
    )

    def column(row):
        spread = jnp.broadcast_to(row, square)
        return jnp.sum(jnp.where(diagonal, spread, 0.0), axis=1, keepdims=True)

    logits = [column(logits_ref[k : k + 1, :]) for k in range(2)]
    ids = [column(ids_ref[k : k + 1, :].astype(jnp.float32)) for k in range(2)]
    lane = lax.broadcasted_iota(jnp.int32, (row_count, LANES), 1)
    expert = (lane % experts).astype(jnp.float32)
    share = jnp.zeros((row_count, LANES), jnp.float32)
    for k in range(2):
        prob = 1.0 / (1.0 + jnp.exp(logits[1 - k] - logits[k]))
        share = share + jnp.where(ids[k] == expert, prob, 0.0)
    high = share.astype(jnp.bfloat16).astype(jnp.float32)
    middle = (share - high).astype(jnp.bfloat16).astype(jnp.float32)
    low = share - high - middle
    piece = lane // experts
    pieces = jnp.where(piece == 0, high, jnp.where(piece == 1, middle, low))
    shared_ref[:, width:] = jnp.where(piece < 3, pieces, 0.0).astype(jnp.bfloat16)


def stack_kernel(fan, *refs):
    out_ref = refs[-1]
    count = refs[0].shape[0]
    if count % 16:
        blocks = [r[...].astype(jnp.float32) for r in refs[:fan]]
        out_ref[...] = jnp.concatenate(blocks, axis=0).astype(out_ref.dtype)
    else:
        for k in range(fan):
            out_ref[k * count : (k + 1) * count] = refs[k][...]


def stack(mine, received, after, flops):
    fan = 1 + len(received)
    return small_call(
        lambda *refs: stack_kernel(fan, *refs),
        "stack",
        jax.ShapeDtypeStruct((fan * mine.shape[0], mine.shape[1]), mine.dtype),
        mine,
        *received,
        after=after,
        flops=flops,
    )


def fold_kernel(places, fan, *refs):
    sources, outs = refs[: len(places)], refs[len(refs) - fan :]
    count, width = outs[0].shape
    for at in range(0, width, STRIP):
        total = 0.0
        for ref, (row, column) in zip(sources, places):
            piece = ref[pl.ds(row, fan * count), pl.ds(column + at, STRIP)]
            total = total + piece.astype(jnp.float32)
        for k, out_ref in enumerate(outs):
            piece = total[k * count : (k + 1) * count]
            out_ref[:, pl.ds(at, STRIP)] = piece.astype(out_ref.dtype)


def fold(sources, shape, types, cost, after=()):
    places = [place for _, *place in sources]
    fan = len(types)
    shape = (shape[0] // fan, shape[1])
    return small_call(
        lambda *refs: fold_kernel(places, fan, *refs),
        "fold",
        [jax.ShapeDtypeStruct(shape, t) for t in types],
        *[source for source, *_ in sources],
        after=after,
        flops=int(cost * GIGA),
    )


def finish_kernel(taken, *refs):
    out_ref = refs[-1]
    at = 0
    for k in range(2):
        total_ref, *received = refs[k * (taken + 1) : (k + 1) * (taken + 1)]
        columns = pl.ds(at, total_ref.shape[1])
        total = total_ref[...]
        for r in received:
            total = total + r[...].astype(jnp.float32)
        out_ref[:, columns] = total.astype(jnp.bfloat16)
        at += total_ref.shape[1]


def per_device(tokens, router_logits, expert_ids, w_gate, w_up, w_down):
    chips = lax.axis_size(("exp", "tp"))
    experts = lax.axis_size(("sect", "exp")) // 4
    bits = chips.bit_length() - 1
    own, model_width = tokens.shape
    width = model_width // 2

    def swap_with(flips):
        return [
            (core * chips + chip, (core ^ flips[2]) * chips + (chip ^ flips[core]))
            for core in range(2)
            for chip in range(chips)
        ]

    def permute(rows, step):
        rows = rows if isinstance(rows, list) else [rows] * len(step)
        return [lax.ppermute(r, AXES, swap_with(flips)) for r, flips in zip(rows, step)]

    core_swap = [(0, 0, 1)]
    steps = [[(1 << k, 1 << k, 0)] for k in range(bits - 1, 3, -1)]
    steps.append([(m, m, 0) for m in (4, 8, 12)])
    steps.append([(2, 1, 0)])
    steps.append([(1, 2, 0)])

    sources = [
        pltpu.with_memory_space_constraint(x, pltpu.HBM)
        for x in (tokens, router_logits.T, expert_ids.T)
    ]
    rows = pl.pallas_call(
        lambda *refs: cut_kernel(experts, *refs),
        in_specs=[HBM] * 3,
        out_specs=[VMEM] * 2,
        out_shape=[
            jax.ShapeDtypeStruct((own, width), tokens.dtype),
            jax.ShapeDtypeStruct((own, width + LANES), tokens.dtype),
        ],
        scratch_shapes=[pltpu.VMEM(x.shape, x.dtype) for x in sources]
        + [pltpu.SemaphoreType.DMA((3,))],
        cost_estimate=pl.CostEstimate(flops=10**6, bytes_accessed=0, transcendentals=0),
        compiler_params=pltpu.CompilerParams(vmem_limit_bytes=2 << 20),
        name="cut",
    )(*sources)
    rows = list(rows)
    flying = [permute(r, steps[0]) for r in rows]
    for k in range(len(steps) - 1):
        for c in range(2):
            rows[c] = stack(rows[c], flying[c], (rows[1 - c],), int(STACK_COST[c][min(k, 1)] * GIGA))
            flying[c] = permute(rows[c], steps[k + 1])
    early = [permute(r, core_swap)[0] for r in rows]
    arrived = [f[0] for f in flying]
    weights, cost = (w_gate, w_up), FFN_COST

    sums = list(pair((rows[0], early[0]), *weights, width, cost[0], (rows[1],)))
    arrived[0], sums[0] = lax.optimization_barrier((arrived[0], sums[0]))
    late = permute(arrived[0], core_swap)[0]
    hidden = [hidden_rows((rows[1], early[1]), *weights, sums, width, cost[1], (arrived[0],))]
    sums = list(pair((arrived[0], late), *weights, width, cost[2], (hidden[0],)))
    arrived[1], sums[0] = lax.optimization_barrier((arrived[1], sums[0]))
    late = permute(arrived[1], core_swap)[0]
    hidden.append(hidden_rows((arrived[1], late), *weights, sums, width, cost[3]))
    parts = (rows[1], early[1], arrived[1], late)

    totals, flying = [], []
    for c in range(2):
        kept, sent = down(experts, hidden, w_down, parts, c, width, cost[4])
        totals.append(kept)
        flying.append(permute([sent], core_swap))
    near, far = steps[-2:]
    count = rows[0].shape[0] // 2
    wide, narrow = jnp.float32, jnp.bfloat16
    inner, outer, passed = [None, None], [None, None], [None, None]
    for c in range(2):
        sources = [(totals[c], 0, 0), (*flying[c], 0, 0)]
        types = (wide, wide, narrow, narrow)
        after = (totals[1],) if c == 0 else (totals[0][0],)
        *kept, inside, outside = fold(sources, (4 * count, width), types, MERGE_COST[0], after)
        totals[c] = kept
        outer[c] = permute(outside, far)
        inner[c] = permute(inside, far)
    for c in range(2):
        after = (totals[0][0],) if c == 0 else (leaving,)
        sources = [(totals[c][1], 0, 0), (*outer[c], 0, 0)]
        (leaving,) = fold(sources, (count, width), (narrow,), MERGE_COST[1], after)
        passed[c] = permute(leaving, near)
    after = (leaving,)
    for c in range(2):
        sources = [(x, 0, 0) for x in (totals[c][0], *inner[c], *passed[c])]
        types = (wide,) + (narrow,) * len(steps[-3])
        totals[c], *sent = fold(sources, (count, width), types, MERGE_COST[2], after)
        flying[c] = permute(sent, steps[-3])
        after = (totals[c],)
    for step in steps[-4::-1]:
        for c in range(2):
            sources = [(x, 0, 0) for x in (totals[c], *flying[c])]
            types = (wide,) + (narrow,) * len(step)
            totals[c], *sent = fold(sources, totals[c].shape, types, MERGE_COST[2])
            flying[c] = permute(sent, step)
    return small_call(
        lambda *refs: finish_kernel(len(flying[0]), *refs),
        "finish",
        jax.ShapeDtypeStruct(tokens.shape, tokens.dtype),
        totals[0],
        *flying[0][::-1],
        totals[1],
        *flying[1][::-1],
    )


def solution(mesh):
    in_specs = (
        P(AXES, None),
        P(AXES, None),
        P(AXES, None),
        P(("sect", "exp"), None, "tp"),
        P(("sect", "exp"), None, "tp"),
        P(("sect", "exp"), "tp", None),
    )
    return jax.shard_map(
        per_device, mesh=mesh, in_specs=in_specs, out_specs=P(AXES, None), check_vma=False
    )
```
